256 devices in a mesh: lat: 8 (over x, y_lo), lon: 32 (over y_hi, z, core).
Axes of the slice: x: 4, y: 4 (y_hi: 2, y_lo: 2; y = y_hi * 2 + y_lo), z: 8, core: 2. Of those that a mesh axis runs over, the one named last changes fastest.
Arguments:
- forcing: float32 [2, 2, 8, 128, 256], P(None, None, None, 'lat', 'lon'), may hold values from -6 to 6
- zonal: float32 [8, 128, 256], P(None, 'lat', 'lon'), may hold values from -0.3 to 0.3
- meridional: float32 [8, 128, 256], P(None, 'lat', 'lon'), may hold values from -0.3 to 0.3
- mixing: float32 [7, 128, 256], P(None, 'lat', 'lon'), may hold values from 0.03 to 0.24
- panel: bfloat16 [32768, 8, 4096], P('lat', None, 'lon'), may hold values from -0.046875 to 0.046875
Outputs:
- adjoint_state: float32 [2, 8, 128, 256], P(None, None, 'lat', 'lon')
- state_grad: float32 [2, 8, 8, 4096], P(None, None, 'lat', 'lon')
- flux_grad: float32 [2, 8, 4096], P(None, 'lat', 'lon')
The draws below stay inside these ranges and needn't reach their ends.
All inputs are finite; a program needn't handle non-finite values.
Results may differ from the reference program's by a relative error of at most 0.0029.
Values may be sent and summed in bfloat16 or wider, within the bound.
A program may use at most 64 MiB of HBM per device.

```python
import math
import jax
import jax.numpy as jnp
from jax import lax

CLAT = 16
CLON = 8
LEV = 8
NLAT = 128
NLON = 256
ORDER = 32768
GCOLS = 4096
N_LAT = 8


def spiked(values, rng, source, target, blocks, factor):
    owner, partner = [(jnp.arange(values.shape[axis_at]) // (values.shape[axis_at] // blocks)).reshape([-1 if axis == axis_at else 1 for axis in range(values.ndim)]) for axis_at in (source, target)]
    chosen = jax.random.permutation(rng, blocks)[partner]
    strong = (owner == chosen) | (owner == (partner + blocks // 2) % blocks)
    return jnp.where(strong, factor * values, values)


def shard_levels(stream_key, dims, cuts, least, largest):
    level, own = 1.0, jax.random.fold_in(stream_key, 6)
    for axis_at, blocks in cuts:
        steps = jnp.exp(jax.random.uniform(jax.random.fold_in(own, axis_at), (blocks,), jnp.float32, least / len(cuts), largest / len(cuts)))
        level = level * jnp.repeat(steps, dims[axis_at] // blocks).reshape([-1 if axis == axis_at else 1 for axis in range(len(dims))])
    return level


def gaussian(key, dims, spread, limit, pieces=(), kind=jnp.bfloat16):
    drawn = jax.random.normal(key, dims, jnp.float32) * spread
    if len(pieces) > 0:
        drawn = shard_levels(key, dims, pieces, -0.22, 0.18) * drawn
    return jnp.clip(drawn, min=-limit, max=limit).astype(kind)


def noise_with(stream_key, extent, width, limit, pieces, heavy, held_as=jnp.bfloat16):
    drawn = width * jax.random.normal(stream_key, extent, jnp.float32)
    if pieces:
        drawn = drawn * shard_levels(stream_key, extent, pieces, -0.22, 0.18)
    return jnp.clip(spiked(drawn, jax.random.fold_in(stream_key, 3), *heavy), -limit, limit).astype(held_as)


def setup_inputs(seed: int = 0) -> dict:
    arg_keys = jax.random.split(jax.random.key(seed), 6)
    return {
        "forcing": gaussian(arg_keys[0], (2, 2, LEV, NLAT, NLON), 1.0, 6.0, ((3, 8), (4, 32)), jnp.float32),
        "zonal": jnp.clip(jax.random.uniform(arg_keys[1], (LEV, NLAT, NLON), jnp.float32, -0.3, 0.3) * shard_levels(arg_keys[1], (LEV, NLAT, NLON), ((1, 8), (2, 32)), -0.4, 0.0), -0.3, 0.3),
        "meridional": jnp.clip(jax.random.uniform(arg_keys[2], (LEV, NLAT, NLON), jnp.float32, -0.3, 0.3) * shard_levels(arg_keys[2], (LEV, NLAT, NLON), ((1, 8), (2, 32)), -0.4, 0.0), -0.3, 0.3),
        "mixing": jnp.clip(jnp.exp(math.log(0.24) - 2.0794415 * jax.random.uniform(arg_keys[3], (LEV - 1, NLAT, NLON), jnp.float32) ** shard_levels(arg_keys[3], (LEV - 1, NLAT, NLON), ((1, 8), (2, 32)), -0.2, 0.2)), 0.03, 0.24),
        "panel": noise_with(arg_keys[4], (ORDER, N_LAT, GCOLS), ORDER ** -0.5, 0.046875, ((0, 8), (2, 32)), (0, 1, 8, 2.0)),
    }


def diffuse(tracer, mixing):
    flow = mixing * (tracer[..., 1:, :, :] - tracer[..., :-1, :, :])
    zeros = jnp.zeros_like(flow[..., :1, :, :])
    return tracer + jnp.concatenate([flow, zeros], -3) - jnp.concatenate([zeros, flow], -3)


def advect(tracer, zonal, merid_masked):
    out_east = jnp.maximum(zonal, 0.0)
    in_west = jnp.roll(jnp.minimum(zonal, 0.0), 1, -1)
    out_north = jnp.maximum(merid_masked, 0.0)
    south_min = jnp.minimum(merid_masked, 0.0)
    in_south = jnp.concatenate([jnp.zeros_like(south_min[:, :1]), south_min[:, :-1]], 1)
    east = jnp.roll(tracer, -1, -1)
    west = jnp.roll(tracer, 1, -1)
    zero_row = jnp.zeros_like(tracer[..., :1, :])
    north = jnp.concatenate([tracer[..., 1:, :], zero_row], -2)
    south = jnp.concatenate([zero_row, tracer[..., :-1, :]], -2)
    return (tracer * (1.0 - out_east + in_west - out_north + in_south)
            + east * out_east - west * in_west + north * out_north - south * in_south)


def to_blocks(values):
    leading = values.shape[:-2]
    shaped = values.reshape(leading + (NLAT // CLAT, CLAT, NLON // CLON, CLON))
    shaped = jnp.swapaxes(shaped, -3, -2)
    return shaped.reshape(leading + (ORDER,))


def reference(forcing, zonal, meridional, mixing, panel):
    top_mask = (jnp.arange(NLAT) < NLAT - 1).astype(meridional.dtype)[None, :, None]
    merid_masked = meridional * top_mask
    lam_one = advect(diffuse(forcing[1], mixing), zonal, merid_masked)
    middle = lam_one + forcing[0]
    adjoint_state = advect(diffuse(middle, mixing), zonal, merid_masked)
    surface = forcing[1][:, 0] + middle[:, 0]
    flux_vec = to_blocks(surface).astype(jnp.bfloat16)
    state_vec = to_blocks(adjoint_state).reshape(2 * LEV, ORDER).astype(jnp.bfloat16)
    vectors = jnp.concatenate([flux_vec, state_vec], 0)
    row_block = ORDER // N_LAT

    def accumulate(total, index):
        start = (index * row_block).astype(jnp.int32)
        rows_part = lax.dynamic_slice_in_dim(panel, start, row_block, 0).reshape(row_block, ORDER)
        vec_part = lax.dynamic_slice_in_dim(vectors, start, row_block, 1)
        return total + jnp.dot(vec_part, rows_part, preferred_element_type=jnp.float32), None

    total, unused = lax.scan(accumulate, jnp.zeros((2 + 2 * LEV, ORDER), jnp.float32),
                             jnp.arange(N_LAT, dtype=jnp.int32))
    total = total.reshape(2 + 2 * LEV, N_LAT, GCOLS)
    flux_grad = total[:2]
    state_grad = total[2:].reshape(2, LEV, N_LAT, GCOLS)
    return (adjoint_state, state_grad, flux_grad)
```

```python
import functools

import jax
import jax.numpy as jnp
from jax import lax
from jax.experimental import pallas as pl
from jax.experimental.pallas import tpu as pltpu
from jax.sharding import PartitionSpec as P

MESH = pl.DeviceIdType.MESH
CHUNKS = 8
GROUP = 4


def kernel(n_lat, n_lon, forcing, zonal, merid, mixing, panel, adj_out, state_out, flux_out,
           raw, pan, msg, halo4, halo8, expand, tiles, own, gathered, partial, arrived, adj_buf,
           in_sem, pan_sem, msg_send, msg_recv, gat_send, gat_recv, red_send, red_recv, out_sem):
    lat, lon = lax.axis_index("lat"), lax.axis_index("lon")
    f32, bf16 = jnp.float32, jnp.bfloat16

    def at(dlat, dlon):
        return {"lat": lax.rem(lat + (dlat + n_lat), n_lat), "lon": lax.rem(lon + (dlon + n_lon), n_lon)}

    barrier = pltpu.get_barrier_semaphore()
    corners = [(1, 1), (1, -1), (-1, 1), (-1, -1)]
    for dlat, dlon in corners:
        pl.semaphore_signal(barrier, inc=1, device_id=at(dlat, dlon), device_id_type=MESH)
    for d in range(1, n_lat):
        pl.semaphore_signal(barrier, inc=1, device_id=at(d, 0), device_id_type=MESH)
    for k in range(1, n_lon):
        pl.semaphore_signal(barrier, inc=1, device_id=at(0, k), device_id_type=MESH)

    loads = [
        pltpu.make_async_copy(forcing, raw.at[0:32], in_sem.at[0]),
        pltpu.make_async_copy(zonal, raw.at[32:40], in_sem.at[1]),
        pltpu.make_async_copy(merid, raw.at[40:48], in_sem.at[2]),
        pltpu.make_async_copy(mixing, raw.at[48:55], in_sem.at[3]),
    ]
    for load in loads:
        load.start()
    rows = panel.shape[0] // CHUNKS
    pan_loads = [
        pltpu.make_async_copy(panel.at[i * rows:(i + 1) * rows], pan.at[i * rows:(i + 1) * rows], pan_sem.at[i])
        for i in range(CHUNKS)
    ]
    for load in pan_loads:
        load.start()

    q = lax.broadcasted_iota(jnp.int32, (128, 1024), 0)
    big = lax.broadcasted_iota(jnp.int32, (128, 1024), 1)
    expand[...] = jnp.where((big >> 3) == q, 1.0, 0.0).astype(bf16)
    row16 = lax.broadcasted_iota(jnp.int32, (16, 128), 0)
    lane16 = lax.broadcasted_iota(jnp.int32, (16, 128), 1)
    for a in range(8):
        tiles[a] = jnp.where((lane16 & 7) == a, 1.0, 0.0).astype(bf16)
    tiles[8] = jnp.where((lane16 & 7) == (row16 >> 1), 1.0, 0.0).astype(bf16)

    lane = lax.broadcasted_iota(jnp.int32, (8, 128), 1)
    sub = lax.broadcasted_iota(jnp.int32, (8, 128), 0)
    li = lane & 15
    first_row, last_row = li == 0, li == 15
    first_col, last_col = sub == 0, sub == 7

    for load in loads:
        load.wait()

    def packed(start, count):
        return jnp.concatenate([raw[start + k] for k in range(count)], axis=1)

    zero_level = jnp.zeros((8, 16), f32)
    obs = [packed(0, 8), packed(8, 8)]
    last = [packed(16, 8), packed(24, 8)]
    z = packed(32, 8)
    vm = jnp.where(last_row & (lat == n_lat - 1), 0.0, packed(40, 8))
    mix = jnp.concatenate([raw[48 + k] for k in range(7)] + [zero_level], axis=1)

    def up(x, s):
        return pltpu.roll(x, s % 128, 1)

    def side(x, s):
        return pltpu.roll(x, s % 8, 0)

    def diffuse(x, m):
        flow = m * (up(x, -16) - x)
        return x + flow - up(flow, 16)

    g = [diffuse(x, mix) for x in last]
    mine = g + [z, vm] + obs + [mix]

    def pack_rows(top):
        total = jnp.zeros((8, 128), f32)
        for n, x in enumerate(mine):
            total = jnp.where((li >> 1) == n, up(x, 2 * n - (14 if top else 0)), total)
        return total

    def pack_cols(right, fields):
        total = jnp.zeros((8, 128), f32)
        for n, x in enumerate(fields):
            total = jnp.where((sub >> 1) == n, side(x, 2 * n - (6 if right else 0)), total)
        return total

    msg[0] = pack_rows(True)
    msg[1] = pack_rows(False)
    msg[2] = pack_cols(True, mine[:4])
    msg[3] = pack_cols(True, mine[4:])
    msg[4] = pack_cols(False, mine[:4])
    msg[5] = pack_cols(False, mine[4:])

    pl.semaphore_wait(barrier, (n_lat - 1) + (n_lon - 1) + 4)

    def row_copy(slot, kind, dlat, dlon):
        return pltpu.make_async_remote_copy(
            src_ref=msg.at[kind], dst_ref=halo4.at[slot], send_sem=msg_send.at[slot], recv_sem=msg_recv.at[slot],
            device_id=at(dlat, dlon), device_id_type=MESH)

    def col_copy(slot, kind, dlon):
        return pltpu.make_async_remote_copy(
            src_ref=msg.at[kind:kind + 2], dst_ref=halo8.at[slot], send_sem=msg_send.at[6 + slot],
            recv_sem=msg_recv.at[6 + slot], device_id=at(0, dlon), device_id_type=MESH)

    halos = [
        row_copy(0, 1, -1, 0), row_copy(3, 0, 1, 0), col_copy(0, 4, -1), col_copy(1, 2, 1),
        row_copy(1, 1, -1, -1), row_copy(2, 1, -1, 1), row_copy(4, 0, 1, -1), row_copy(5, 0, 1, 1),
    ]
    for copy in halos:
        copy.start()

    def advect(x, north, south, east, west, c):
        p, nw, qn, ns = c
        return x * (1.0 - p + nw - qn + ns) + east * p - west * nw + north * qn - south * ns

    def coefs(zc, z_west, v, v_south):
        return (jnp.maximum(zc, 0.0), jnp.minimum(z_west, 0.0), jnp.maximum(v, 0.0), jnp.minimum(v_south, 0.0))

    for copy in halos:
        copy.wait_recv()

    def rows_of(slot, n, north):
        return up(halo4[slot], -2 * n if north else 14 - 2 * n)

    def cols_of(slot, n):
        return side(halo8[slot, n // 4], -2 * (n % 4) if slot == 0 else 6 - 2 * (n % 4))

    N = [rows_of(0, n, True) for n in range(7)]
    S = [rows_of(3, n, False) for n in range(7)]
    NE = [rows_of(1, n, True) for n in range(4)]
    NW = [rows_of(2, n, True) for n in range(4)]
    SE = [rows_of(4, n, False) for n in range(4)]
    SW = [rows_of(5, n, False) for n in range(4)]
    E = [cols_of(0, n) for n in range(7)]
    W = [cols_of(1, n) for n in range(7)]

    def north_of(x, xn):
        return jnp.where(last_row, up(xn, 15), up(x, -1))

    def south_of(x, xs):
        return jnp.where(first_row, up(xs, -15), up(x, 1))

    def east_of(x, xe):
        return side(jnp.where(first_col, xe, x), -1)

    def west_of(x, xw):
        return side(jnp.where(last_col, xw, x), 1)

    def middle(me, n_, s_, e_, w_):
        c = coefs(me[2], west_of(me[2], w_[2]), me[3], south_of(me[3], s_[3]))
        return c, [
            advect(me[s], north_of(me[s], n_[s]), south_of(me[s], s_[s]), east_of(me[s], e_[s]), west_of(me[s], w_[s]), c)
            + me[4 + s]
            for s in range(2)
        ]

    coef, mid = middle(mine, N, S, E, W)
    mid_n = middle(N, N, mine, NE, NW)[1]
    mid_s = middle(S, mine, S, SE, SW)[1]
    mid_e = middle(E, NE, SE, E, mine)[1]
    mid_w = middle(W, NW, SW, mine, W)[1]
    surface = [last[s] + mid[s] for s in range(2)]
    adjoint = []
    for s in range(2):
        d = diffuse(mid[s], mix)
        dn, ds = diffuse(mid_n[s], N[6]), diffuse(mid_s[s], S[6])
        de, dw = diffuse(mid_e[s], E[6]), diffuse(mid_w[s], W[6])
        adjoint.append(advect(d, north_of(d, dn), south_of(d, ds), east_of(d, de), west_of(d, dw), coef))

    x = jnp.concatenate([adjoint[0], adjoint[1]], axis=0).astype(bf16)
    y = jnp.dot(x, expand[...], preferred_element_type=f32)
    xs = jnp.concatenate(surface, axis=0).astype(bf16)
    ys = jnp.dot(xs, expand[:, 0:128], preferred_element_type=f32)
    keep = (lax.broadcasted_iota(jnp.int32, (16, 128), 1) & 7) == (lax.broadcasted_iota(jnp.int32, (16, 128), 0) & 7)
    blocks = [jnp.where(keep, y[:, k * 128:(k + 1) * 128], 0.0).astype(bf16) for k in range(8)]
    stacked = jnp.concatenate(blocks, axis=0)
    c_row = lax.broadcasted_iota(jnp.int32, (16, 128), 0)
    c_col = lax.broadcasted_iota(jnp.int32, (16, 128), 1)
    pick = (((c_col >> 4) == (c_row & 7)) & (((c_col >> 3) & 1) == (c_row >> 3)))
    state_vec = jnp.dot(jnp.where(pick, 1.0, 0.0).astype(bf16), stacked, preferred_element_type=f32)
    f_row = lax.broadcasted_iota(jnp.int32, (16, 16), 0)
    f_col = lax.broadcasted_iota(jnp.int32, (16, 16), 1)
    pick_f = jnp.where((f_col >> 3) == (f_row & 1), 1.0, 0.0).astype(bf16)
    flux_vec = jnp.dot(pick_f, jnp.where(keep, ys, 0.0).astype(bf16), preferred_element_type=f32)
    own[...] = jnp.concatenate([state_vec, flux_vec], axis=0).astype(bf16)

    def gather_copy(k):
        return pltpu.make_async_remote_copy(
            src_ref=own, dst_ref=gathered.at[k], send_sem=gat_send.at[k], recv_sem=gat_recv.at[k],
            device_id=at(0, k), device_id_type=MESH)

    for k in range(1, n_lon):
        gather_copy(k).start()

    for s in range(2):
        for k in range(8):
            adj_buf[s * 8 + k] = up(adjoint[s], -16 * k)[:, 0:16]
    adj_copy = pltpu.make_async_copy(adj_buf, adj_out, out_sem.at[0])
    adj_copy.start()

    gathered[0] = own[...]
    for load in pan_loads:
        load.wait()

    def piece(k, acc):
        w = jnp.dot(gathered[k], expand[...], preferred_element_type=f32).astype(bf16)
        left = jnp.concatenate(
            [jnp.concatenate([w[0:16, b * 128:(b + 1) * 128] * tiles[a] for b in range(8)], axis=1) for a in range(8)]
            + [jnp.concatenate([w[16:32, b * 128:(b + 1) * 128] * tiles[8] for b in range(8)], axis=1)], axis=0)
        source = lax.rem(lon - k + n_lon, n_lon)
        right = pan[pl.ds(source * 128, 128)].reshape(1024, 128)
        return acc + jnp.dot(left, right, preferred_element_type=f32)

    acc = piece(0, jnp.zeros((144, 128), f32))
    for k in range(1, GROUP):
        gather_copy(k).wait_recv()
        acc = piece(k, acc)

    def group(i, acc):
        for j in range(GROUP):
            k = i * GROUP + j
            gather_copy(k).wait_recv()
            acc = piece(k, acc)
        return acc

    acc = lax.fori_loop(1, n_lon // GROUP, group, acc)

    for a in range(n_lat):
        partial[a, 0:16] = acc[a * 16:(a + 1) * 16]
        partial[a, 16:18] = acc[128 + 2 * a:130 + 2 * a]

    def reduce_copy(d):
        return pltpu.make_async_remote_copy(
            src_ref=partial.at[lax.rem(lat + d, n_lat)], dst_ref=arrived.at[d - 1], send_sem=red_send.at[d - 1],
            recv_sem=red_recv.at[d - 1], device_id=at(d, 0), device_id_type=MESH)

    for d in range(1, n_lat):
        reduce_copy(d).start()
    for copy in halos:
        copy.wait_send()
    for k in range(1, n_lon):
        gather_copy(k).wait_send()
    total = partial[lat]
    for d in range(1, n_lat):
        reduce_copy(d).wait_recv()
        total = total + arrived[d - 1]
    state_out[...] = total[0:16]
    flux_out[...] = total[16:18]
    for d in range(1, n_lat):
        reduce_copy(d).wait_send()
    adj_copy.wait()


def shards(n_lat, n_lon, forcing, zonal, meridional, mixing, panel):
    def turned(x):
        return jnp.swapaxes(x, -1, -2).reshape((-1, x.shape[-1], x.shape[-2]))

    f32, bf16 = jnp.float32, jnp.bfloat16
    rows = panel.shape[0]
    hbm, vmem = pl.BlockSpec(memory_space=pl.ANY), pl.BlockSpec(memory_space=pltpu.VMEM)
    dma = pltpu.SemaphoreType.DMA
    adj, state, flux = pl.pallas_call(
        functools.partial(kernel, n_lat, n_lon),
        out_shape=(
            jax.ShapeDtypeStruct((16, 8, 16), f32),
            jax.ShapeDtypeStruct((16, 128), f32),
            jax.ShapeDtypeStruct((2, 128), f32),
        ),
        in_specs=[hbm] * 5,
        out_specs=(hbm, vmem, vmem),
        scratch_shapes=[
            pltpu.VMEM((55, 8, 16), f32),
            pltpu.VMEM((rows, 8, 128), bf16),
            pltpu.VMEM((6, 8, 128), f32),
            pltpu.VMEM((6, 8, 128), f32),
            pltpu.VMEM((2, 2, 8, 128), f32),
            pltpu.VMEM((128, 1024), bf16),
            pltpu.VMEM((9, 16, 128), bf16),
            pltpu.VMEM((32, 128), bf16),
            pltpu.VMEM((n_lon, 32, 128), bf16),
            pltpu.VMEM((n_lat, 24, 128), f32),
            pltpu.VMEM((n_lat - 1, 24, 128), f32),
            pltpu.VMEM((16, 8, 16), f32),
            dma((4,)), dma((CHUNKS,)), dma((8,)), dma((8,)), dma((n_lon,)), dma((n_lon,)),
            dma((n_lat - 1,)), dma((n_lat - 1,)), dma((1,)),
        ],
        compiler_params=pltpu.CompilerParams(
            collective_id=0, has_side_effects=True, vmem_limit_bytes=48 * 1024 * 1024),
    )(turned(forcing), turned(zonal), turned(meridional), turned(mixing), panel)
    adjoint = jnp.swapaxes(adj.reshape(2, 8, 8, 16), 2, 3)
    return adjoint, state.reshape(2, 8, 1, 128), flux.reshape(2, 1, 128)


def solution(mesh):
    return jax.shard_map(
        functools.partial(shards, mesh.shape["lat"], mesh.shape["lon"]),
        mesh=mesh,
        in_specs=(
            P(None, None, None, "lat", "lon"),
            P(None, "lat", "lon"),
            P(None, "lat", "lon"),
            P(None, "lat", "lon"),
            P("lat", None, "lon"),
        ),
        out_specs=(P(None, None, "lat", "lon"), P(None, None, "lat", "lon"), P(None, "lat", "lon")),
        check_vma=False,
    )
```

```python
import functools

import jax
import jax.numpy as jnp
from jax import lax
from jax.experimental import pallas as pl
from jax.experimental.pallas import tpu as pltpu
from jax.sharding import PartitionSpec as P

MESH = pl.DeviceIdType.MESH
CHUNKS = 8


def kernel(n_lat, n_lon, forcing, zonal, merid, mixing, panel, adj_out, state_out, flux_out,
           raw, pan, msg, halo4, halo8, expand, wide, own, gathered, partial, arrived, adj_buf,
           in_sem, pan_sem, msg_send, msg_recv, gat_send, gat_recv, red_send, red_recv, out_sem):
    lat, lon = lax.axis_index("lat"), lax.axis_index("lon")
    f32, bf16 = jnp.float32, jnp.bfloat16

    def at(dlat, dlon):
        return {"lat": lax.rem(lat + (dlat + n_lat), n_lat), "lon": lax.rem(lon + (dlon + n_lon), n_lon)}

    barrier = pltpu.get_barrier_semaphore()
    corners = [(1, 1), (1, -1), (-1, 1), (-1, -1)]
    for dlat, dlon in corners:
        pl.semaphore_signal(barrier, inc=1, device_id=at(dlat, dlon), device_id_type=MESH)
    for d in range(1, n_lat):
        pl.semaphore_signal(barrier, inc=1, device_id=at(d, 0), device_id_type=MESH)
    for k in range(1, n_lon):
        pl.semaphore_signal(barrier, inc=1, device_id=at(0, k), device_id_type=MESH)

    loads = [
        pltpu.make_async_copy(forcing, raw.at[0:32], in_sem.at[0]),
        pltpu.make_async_copy(zonal, raw.at[32:40], in_sem.at[1]),
        pltpu.make_async_copy(merid, raw.at[40:48], in_sem.at[2]),
        pltpu.make_async_copy(mixing, raw.at[48:55], in_sem.at[3]),
    ]
    for load in loads:
        load.start()
    rows = panel.shape[0] // CHUNKS
    pan_loads = [
        pltpu.make_async_copy(panel.at[i * rows:(i + 1) * rows], pan.at[i * rows:(i + 1) * rows], pan_sem.at[i])
        for i in range(CHUNKS)
    ]
    for load in pan_loads:
        load.start()

    q = lax.broadcasted_iota(jnp.int32, (128, 1024), 0)
    big = lax.broadcasted_iota(jnp.int32, (128, 1024), 1)
    expand[...] = jnp.where((big >> 3) == q, 1.0, 0.0).astype(bf16)
    lane = lax.broadcasted_iota(jnp.int32, (8, 128), 1)
    sub = lax.broadcasted_iota(jnp.int32, (8, 128), 0)
    li = lane & 15
    first_row, last_row = li == 0, li == 15
    first_col, last_col = sub == 0, sub == 7

    for load in loads:
        load.wait()

    def packed(start, count):
        return jnp.concatenate([raw[start + k] for k in range(count)], axis=1)

    zero_level = jnp.zeros((8, 16), f32)
    obs = [packed(0, 8), packed(8, 8)]
    last = [packed(16, 8), packed(24, 8)]
    z = packed(32, 8)
    vm = jnp.where(last_row & (lat == n_lat - 1), 0.0, packed(40, 8))
    mix = jnp.concatenate([raw[48 + k] for k in range(7)] + [zero_level], axis=1)

    def up(x, s):
        return pltpu.roll(x, s % 128, 1)

    def side(x, s):
        return pltpu.roll(x, s % 8, 0)

    def diffuse(x, m):
        flow = m * (up(x, -16) - x)
        return x + flow - up(flow, 16)

    g = [diffuse(x, mix) for x in last]
    mine = g + [z, vm] + obs + [mix]

    def pack_rows(top):
        total = jnp.zeros((8, 128), f32)
        for n, x in enumerate(mine):
            total = jnp.where((li >> 1) == n, up(x, 2 * n - (14 if top else 0)), total)
        return total

    def pack_cols(right, fields):
        total = jnp.zeros((8, 128), f32)
        for n, x in enumerate(fields):
            total = jnp.where((sub >> 1) == n, side(x, 2 * n - (6 if right else 0)), total)
        return total

    msg[0] = pack_rows(True)
    msg[1] = pack_rows(False)
    msg[2] = pack_cols(True, mine[:4])
    msg[3] = pack_cols(True, mine[4:])
    msg[4] = pack_cols(False, mine[:4])
    msg[5] = pack_cols(False, mine[4:])

    pl.semaphore_wait(barrier, (n_lat - 1) + (n_lon - 1) + 4)

    def row_copy(slot, kind, dlat, dlon):
        return pltpu.make_async_remote_copy(
            src_ref=msg.at[kind], dst_ref=halo4.at[slot], send_sem=msg_send.at[slot], recv_sem=msg_recv.at[slot],
            device_id=at(dlat, dlon), device_id_type=MESH)

    def col_copy(slot, kind, dlon):
        return pltpu.make_async_remote_copy(
            src_ref=msg.at[kind:kind + 2], dst_ref=halo8.at[slot], send_sem=msg_send.at[6 + slot],
            recv_sem=msg_recv.at[6 + slot], device_id=at(0, dlon), device_id_type=MESH)

    halos = [
        row_copy(0, 1, -1, 0), row_copy(3, 0, 1, 0), col_copy(0, 4, -1), col_copy(1, 2, 1),
        row_copy(1, 1, -1, -1), row_copy(2, 1, -1, 1), row_copy(4, 0, 1, -1), row_copy(5, 0, 1, 1),
    ]
    for copy in halos:
        copy.start()

    def relayout(begin, end):
        for i in range(begin, end):
            pan_loads[i].wait()

            def turn(j, carry):
                at_row = i * rows + j * 128
                wide[pl.ds(at_row, 128), :] = pan[pl.ds(at_row, 128)].reshape(128, 1024)
                return carry

            lax.fori_loop(0, rows // 128, turn, 0)

    def advect(x, north, south, east, west, c):
        p, nw, qn, ns = c
        return x * (1.0 - p + nw - qn + ns) + east * p - west * nw + north * qn - south * ns

    def coefs(zc, z_west, v, v_south):
        return (jnp.maximum(zc, 0.0), jnp.minimum(z_west, 0.0), jnp.maximum(v, 0.0), jnp.minimum(v_south, 0.0))

    relayout(0, CHUNKS)

    for copy in halos:
        copy.wait_recv()

    def rows_of(slot, n, north):
        return up(halo4[slot], -2 * n if north else 14 - 2 * n)

    def cols_of(slot, n):
        return side(halo8[slot, n // 4], -2 * (n % 4) if slot == 0 else 6 - 2 * (n % 4))

    N = [rows_of(0, n, True) for n in range(7)]
    S = [rows_of(3, n, False) for n in range(7)]
    NE = [rows_of(1, n, True) for n in range(4)]
    NW = [rows_of(2, n, True) for n in range(4)]
    SE = [rows_of(4, n, False) for n in range(4)]
    SW = [rows_of(5, n, False) for n in range(4)]
    E = [cols_of(0, n) for n in range(7)]
    W = [cols_of(1, n) for n in range(7)]

    def north_of(x, xn):
        return jnp.where(last_row, up(xn, 15), up(x, -1))

    def south_of(x, xs):
        return jnp.where(first_row, up(xs, -15), up(x, 1))

    def east_of(x, xe):
        return side(jnp.where(first_col, xe, x), -1)

    def west_of(x, xw):
        return side(jnp.where(last_col, xw, x), 1)

    def middle(me, n_, s_, e_, w_):
        c = coefs(me[2], west_of(me[2], w_[2]), me[3], south_of(me[3], s_[3]))
        return c, [
            advect(me[s], north_of(me[s], n_[s]), south_of(me[s], s_[s]), east_of(me[s], e_[s]), west_of(me[s], w_[s]), c)
            + me[4 + s]
            for s in range(2)
        ]

    coef, mid = middle(mine, N, S, E, W)
    mid_n = middle(N, N, mine, NE, NW)[1]
    mid_s = middle(S, mine, S, SE, SW)[1]
    mid_e = middle(E, NE, SE, E, mine)[1]
    mid_w = middle(W, NW, SW, mine, W)[1]
    surface = [last[s] + mid[s] for s in range(2)]
    adjoint = []
    for s in range(2):
        d = diffuse(mid[s], mix)
        dn, ds = diffuse(mid_n[s], N[6]), diffuse(mid_s[s], S[6])
        de, dw = diffuse(mid_e[s], E[6]), diffuse(mid_w[s], W[6])
        adjoint.append(advect(d, north_of(d, dn), south_of(d, ds), east_of(d, de), west_of(d, dw), coef))

    x = jnp.concatenate([adjoint[0], adjoint[1]], axis=0).astype(bf16)
    y = jnp.dot(x, expand[...], preferred_element_type=f32)
    xs = jnp.concatenate(surface, axis=0).astype(bf16)
    ys = jnp.dot(xs, expand[:, 0:128], preferred_element_type=f32)
    keep = (lax.broadcasted_iota(jnp.int32, (16, 128), 1) & 7) == (lax.broadcasted_iota(jnp.int32, (16, 128), 0) & 7)
    blocks = [jnp.where(keep, y[:, k * 128:(k + 1) * 128], 0.0).astype(bf16) for k in range(8)]
    stacked = jnp.concatenate(blocks, axis=0)
    c_row = lax.broadcasted_iota(jnp.int32, (16, 128), 0)
    c_col = lax.broadcasted_iota(jnp.int32, (16, 128), 1)
    pick = (((c_col >> 4) == (c_row & 7)) & (((c_col >> 3) & 1) == (c_row >> 3)))
    state_vec = jnp.dot(jnp.where(pick, 1.0, 0.0).astype(bf16), stacked, preferred_element_type=f32)
    f_row = lax.broadcasted_iota(jnp.int32, (16, 16), 0)
    f_col = lax.broadcasted_iota(jnp.int32, (16, 16), 1)
    pick_f = jnp.where((f_col >> 3) == (f_row & 1), 1.0, 0.0).astype(bf16)
    flux_vec = jnp.dot(pick_f, jnp.where(keep, ys, 0.0).astype(bf16), preferred_element_type=f32)
    own[...] = jnp.concatenate([state_vec, flux_vec], axis=0).astype(bf16)

    def gather_copy(k):
        return pltpu.make_async_remote_copy(
            src_ref=own, dst_ref=gathered.at[lon], send_sem=gat_send.at[k], recv_sem=gat_recv.at[lon],
            device_id=at(0, k), device_id_type=MESH)

    def gather_wait(l):
        return pltpu.make_async_remote_copy(
            src_ref=own, dst_ref=gathered.at[l], send_sem=gat_send.at[0], recv_sem=gat_recv.at[l],
            device_id=at(0, 1), device_id_type=MESH)

    for k in range(1, n_lon):
        gather_copy(k).start()

    for s in range(2):
        for k in range(8):
            adj_buf[s * 8 + k] = up(adjoint[s], -16 * k)[:, 0:16]
    adj_copy = pltpu.make_async_copy(adj_buf, adj_out, out_sem.at[0])
    adj_copy.start()

    gathered[lon] = own[...]
    acc = None
    for pair in range(n_lon // 2):
        first = pair // 2 * 2 + pair % 2 * (n_lon // 2)
        for l in (first, first + 1):
            @pl.when(lon != l)
            def _():
                gather_wait(l).wait_recv()
        left = jnp.concatenate([gathered[first], gathered[first + 1]], axis=1)
        term = jnp.dot(left, wide[first * 128:(first + 2) * 128, :], preferred_element_type=f32)
        acc = term if acc is None else acc + term

    for a in range(n_lat):
        partial[a] = acc[0:24, a * 128:(a + 1) * 128]

    def reduce_copy(d):
        return pltpu.make_async_remote_copy(
            src_ref=partial.at[lax.rem(lat + d, n_lat)], dst_ref=arrived.at[d - 1], send_sem=red_send.at[d - 1],
            recv_sem=red_recv.at[d - 1], device_id=at(d, 0), device_id_type=MESH)

    for d in range(1, n_lat):
        reduce_copy(d).start()
    for copy in halos:
        copy.wait_send()
    for k in range(1, n_lon):
        gather_copy(k).wait_send()
    total = partial[lat]
    for d in range(1, n_lat):
        reduce_copy(d).wait_recv()
        total = total + arrived[d - 1]
    state_out[...] = total[0:16]
    flux_out[...] = total[16:18]
    for d in range(1, n_lat):
        reduce_copy(d).wait_send()
    adj_copy.wait()


def shards(n_lat, n_lon, forcing, zonal, meridional, mixing, panel):
    def turned(x):
        return jnp.swapaxes(x, -1, -2).reshape((-1, x.shape[-1], x.shape[-2]))

    f32, bf16 = jnp.float32, jnp.bfloat16
    rows = panel.shape[0]
    hbm, vmem = pl.BlockSpec(memory_space=pltpu.HBM), pl.BlockSpec(memory_space=pltpu.VMEM)
    dma = pltpu.SemaphoreType.DMA
    adj, state, flux = pl.pallas_call(
        functools.partial(kernel, n_lat, n_lon),
        out_shape=(
            jax.ShapeDtypeStruct((16, 8, 16), f32),
            jax.ShapeDtypeStruct((16, 128), f32),
            jax.ShapeDtypeStruct((2, 128), f32),
        ),
        in_specs=[hbm] * 5,
        out_specs=(hbm, vmem, vmem),
        scratch_shapes=[
            pltpu.VMEM((55, 8, 16), f32),
            pltpu.VMEM((rows, 8, 128), bf16),
            pltpu.VMEM((6, 8, 128), f32),
            pltpu.VMEM((6, 8, 128), f32),
            pltpu.VMEM((2, 2, 8, 128), f32),
            pltpu.VMEM((128, 1024), bf16),
            pltpu.VMEM((rows, 1024), bf16),
            pltpu.VMEM((32, 128), bf16),
            pltpu.VMEM((n_lon, 32, 128), bf16),
            pltpu.VMEM((n_lat, 24, 128), f32),
            pltpu.VMEM((n_lat - 1, 24, 128), f32),
            pltpu.VMEM((16, 8, 16), f32),
            dma((4,)), dma((CHUNKS,)), dma((8,)), dma((8,)), dma((n_lon,)), dma((n_lon,)),
            dma((n_lat - 1,)), dma((n_lat - 1,)), dma((1,)),
        ],
        compiler_params=pltpu.CompilerParams(
            collective_id=0, has_side_effects=True, vmem_limit_bytes=56 * 1024 * 1024),
    )(turned(forcing), turned(zonal), turned(meridional), turned(mixing), panel)
    adjoint = jnp.swapaxes(adj.reshape(2, 8, 8, 16), 2, 3)
    return adjoint, state.reshape(2, 8, 1, 128), flux.reshape(2, 1, 128)


def solution(mesh):
    return jax.shard_map(
        functools.partial(shards, mesh.shape["lat"], mesh.shape["lon"]),
        mesh=mesh,
        in_specs=(
            P(None, None, None, "lat", "lon"),
            P(None, "lat", "lon"),
            P(None, "lat", "lon"),
            P(None, "lat", "lon"),
            P("lat", None, "lon"),
        ),
        out_specs=(P(None, None, "lat", "lon"), P(None, None, "lat", "lon"), P(None, "lat", "lon")),
        check_vma=False,
    )
```

```python
import functools

import jax
import jax.numpy as jnp
from jax import lax
from jax.experimental import pallas as pl
from jax.experimental.pallas import tpu as pltpu
from jax.sharding import PartitionSpec as P

MESH = pl.DeviceIdType.MESH
CHUNKS = 8
LIMIT = 55200


def kernel(n_lat, n_lon, forcing, zonal, merid, mixing, panel, adj_out, sum_out,
           raw, pan, msg, halo4, halo8, expand, wide, own, gathered, partial, arrived,
           in_sem, pan_sem, msg_send, msg_recv, gat_send, gat_recv, red_send, red_recv):
    lat, lon = lax.axis_index("lat"), lax.axis_index("lon")
    f32, bf16 = jnp.float32, jnp.bfloat16

    def at(dlat, dlon):
        return {"lat": lax.rem(lat + (dlat + n_lat), n_lat), "lon": lax.rem(lon + (dlon + n_lon), n_lon)}

    barrier = pltpu.get_barrier_semaphore()
    corners = [(1, 1), (1, -1), (-1, 1), (-1, -1)]
    for dlat, dlon in corners:
        pl.semaphore_signal(barrier, inc=1, device_id=at(dlat, dlon), device_id_type=MESH)
    for d in range(1, n_lat):
        pl.semaphore_signal(barrier, inc=1, device_id=at(d, 0), device_id_type=MESH)
    for k in range(1, n_lon):
        pl.semaphore_signal(barrier, inc=1, device_id=at(0, k), device_id_type=MESH)

    loads = [
        pltpu.make_async_copy(forcing, raw.at[0:32], in_sem.at[0]),
        pltpu.make_async_copy(zonal, raw.at[32:40], in_sem.at[1]),
        pltpu.make_async_copy(merid, raw.at[40:48], in_sem.at[2]),
        pltpu.make_async_copy(mixing, raw.at[48:55], in_sem.at[3]),
    ]
    for load in loads:
        load.start()
    rows = panel.shape[0] // CHUNKS
    pan_loads = [
        pltpu.make_async_copy(panel.at[i * rows:(i + 1) * rows], pan.at[i * rows:(i + 1) * rows], pan_sem.at[i])
        for i in range(CHUNKS)
    ]
    for load in pan_loads:
        load.start()

    q = lax.broadcasted_iota(jnp.int32, (128, 1024), 0)
    big = lax.broadcasted_iota(jnp.int32, (128, 1024), 1)
    expand[...] = jnp.where((big >> 3) == q, 1.0, 0.0).astype(bf16)
    lane = lax.broadcasted_iota(jnp.int32, (8, 128), 1)
    sub = lax.broadcasted_iota(jnp.int32, (8, 128), 0)
    li = lane & 15
    first_row, last_row = li == 0, li == 15
    first_col, last_col = sub == 0, sub == 7

    for load in loads:
        load.wait()

    def packed(start, count):
        return jnp.concatenate([raw[start + k] for k in range(count)], axis=1)

    zero_level = jnp.zeros((8, 16), f32)
    obs = [packed(0, 8), packed(8, 8)]
    last = [packed(16, 8), packed(24, 8)]
    z = packed(32, 8)
    vm = jnp.where(last_row & (lat == n_lat - 1), 0.0, packed(40, 8))
    mix = jnp.concatenate([raw[48 + k] for k in range(7)] + [zero_level], axis=1)

    def up(x, s):
        return pltpu.roll(x, s % 128, 1)

    def side(x, s):
        return pltpu.roll(x, s % 8, 0)

    def diffuse(x, m):
        flow = m * (up(x, -16) - x)
        return x + flow - up(flow, 16)

    g = [diffuse(x, mix) for x in last]
    mine = g + [z, vm] + obs + [mix]

    def pack_rows(top):
        total = jnp.zeros((8, 128), f32)
        for n, x in enumerate(mine):
            total = jnp.where((li >> 1) == n, up(x, 2 * n - (14 if top else 0)), total)
        return total

    def pack_cols(right, fields):
        total = jnp.zeros((8, 128), f32)
        for n, x in enumerate(fields):
            total = jnp.where((sub >> 1) == n, side(x, 2 * n - (6 if right else 0)), total)
        return total

    msg[0] = pack_rows(True)
    msg[1] = pack_rows(False)
    msg[2] = pack_cols(True, mine[:4])
    msg[3] = pack_cols(True, mine[4:])
    msg[4] = pack_cols(False, mine[:4])
    msg[5] = pack_cols(False, mine[4:])

    pl.semaphore_wait(barrier, (n_lat - 1) + (n_lon - 1) + 4)

    def row_copy(slot, kind, dlat, dlon):
        return pltpu.make_async_remote_copy(
            src_ref=msg.at[kind], dst_ref=halo4.at[slot], send_sem=msg_send.at[slot], recv_sem=msg_recv.at[slot],
            device_id=at(dlat, dlon), device_id_type=MESH)

    def col_copy(slot, kind, dlon):
        return pltpu.make_async_remote_copy(
            src_ref=msg.at[kind:kind + 2], dst_ref=halo8.at[slot], send_sem=msg_send.at[6 + slot],
            recv_sem=msg_recv.at[6 + slot], device_id=at(0, dlon), device_id_type=MESH)

    halos = [
        row_copy(0, 1, -1, 0), row_copy(3, 0, 1, 0), col_copy(0, 4, -1), col_copy(1, 2, 1),
        row_copy(1, 1, -1, -1), row_copy(2, 1, -1, 1), row_copy(4, 0, 1, -1), row_copy(5, 0, 1, 1),
    ]
    for copy in halos:
        copy.start()

    def relayout(begin, end):
        for i in range(begin, end):
            pan_loads[i].wait()

            def turn(j, carry):
                at_row = i * rows + j * 128
                wide[pl.ds(at_row, 128), :] = pan[pl.ds(at_row, 128)].reshape(128, 1024)
                return carry

            lax.fori_loop(0, rows // 128, turn, 0)

    def advect(x, north, south, east, west, c):
        p, nw, qn, ns = c
        return x * (1.0 - p + nw - qn + ns) + east * p - west * nw + north * qn - south * ns

    def coefs(zc, z_west, v, v_south):
        return (jnp.maximum(zc, 0.0), jnp.minimum(z_west, 0.0), jnp.maximum(v, 0.0), jnp.minimum(v_south, 0.0))

    relayout(0, CHUNKS)

    for copy in halos:
        copy.wait_recv()

    def rows_of(slot, n, north):
        return up(halo4[slot], -2 * n if north else 14 - 2 * n)

    def cols_of(slot, n):
        return side(halo8[slot, n // 4], -2 * (n % 4) if slot == 0 else 6 - 2 * (n % 4))

    N = [rows_of(0, n, True) for n in range(7)]
    S = [rows_of(3, n, False) for n in range(7)]
    NE = [rows_of(1, n, True) for n in range(4)]
    NW = [rows_of(2, n, True) for n in range(4)]
    SE = [rows_of(4, n, False) for n in range(4)]
    SW = [rows_of(5, n, False) for n in range(4)]
    E = [cols_of(0, n) for n in range(7)]
    W = [cols_of(1, n) for n in range(7)]

    def north_of(x, xn):
        return jnp.where(last_row, up(xn, 15), up(x, -1))

    def south_of(x, xs):
        return jnp.where(first_row, up(xs, -15), up(x, 1))

    def east_of(x, xe):
        return side(jnp.where(first_col, xe, x), -1)

    def west_of(x, xw):
        return side(jnp.where(last_col, xw, x), 1)

    def middle(me, n_, s_, e_, w_):
        c = coefs(me[2], west_of(me[2], w_[2]), me[3], south_of(me[3], s_[3]))
        return c, [
            advect(me[s], north_of(me[s], n_[s]), south_of(me[s], s_[s]), east_of(me[s], e_[s]), west_of(me[s], w_[s]), c)
            + me[4 + s]
            for s in range(2)
        ]

    coef, mid = middle(mine, N, S, E, W)
    mid_n = middle(N, N, mine, NE, NW)[1]
    mid_s = middle(S, mine, S, SE, SW)[1]
    mid_e = middle(E, NE, SE, E, mine)[1]
    mid_w = middle(W, NW, SW, mine, W)[1]
    surface = [last[s] + mid[s] for s in range(2)]
    adjoint = []
    for s in range(2):
        d = diffuse(mid[s], mix)
        dn, ds = diffuse(mid_n[s], N[6]), diffuse(mid_s[s], S[6])
        de, dw = diffuse(mid_e[s], E[6]), diffuse(mid_w[s], W[6])
        adjoint.append(advect(d, north_of(d, dn), south_of(d, ds), east_of(d, de), west_of(d, dw), coef))

    x = jnp.concatenate([adjoint[0], adjoint[1]], axis=0).astype(bf16)
    y = jnp.dot(x, expand[...], preferred_element_type=f32)
    xs = jnp.concatenate(surface, axis=0).astype(bf16)
    ys = jnp.dot(xs, expand[:, 0:128], preferred_element_type=f32)
    keep = (lax.broadcasted_iota(jnp.int32, (16, 128), 1) & 7) == (lax.broadcasted_iota(jnp.int32, (16, 128), 0) & 7)
    blocks = [jnp.where(keep, y[:, k * 128:(k + 1) * 128], 0.0).astype(bf16) for k in range(8)]
    stacked = jnp.concatenate(blocks, axis=0)
    c_row = lax.broadcasted_iota(jnp.int32, (18, 128), 0)
    c_col = lax.broadcasted_iota(jnp.int32, (18, 128), 1)
    pick = (c_row < 16) & ((c_col >> 4) == (c_row & 7)) & (((c_col >> 3) & 1) == (c_row >> 3))
    f_row = lax.broadcasted_iota(jnp.int32, (18, 16), 0)
    f_col = lax.broadcasted_iota(jnp.int32, (18, 16), 1)
    pick_f = (f_col >> 3) == (f_row - 16)
    vec = jnp.dot(jnp.where(pick, 1.0, 0.0).astype(bf16), stacked, preferred_element_type=f32)
    vec = vec + jnp.dot(
        jnp.where(pick_f, 1.0, 0.0).astype(bf16), jnp.where(keep, ys, 0.0).astype(bf16), preferred_element_type=f32)
    own[...] = vec.astype(bf16)

    half = n_lon // 2
    core, ring, column = lax.rem(lon, 2), lax.rem(lon // 2, half // 2), lon // half

    def other(dz, dy):
        return lax.rem(column + dy, 2) * half + lax.rem(ring + dz, half // 2) * 2 + core

    mate = lon + 1 - 2 * core
    peers = [(dz, dy) for dz in range(half // 2) for dy in range(2) if dz + dy > 0]
    peers = peers[1:] + peers[:1]

    def piece_copy(source, slot, send, target):
        return pltpu.make_async_remote_copy(
            src_ref=source, dst_ref=gathered.at[slot], send_sem=gat_send.at[send], recv_sem=gat_recv.at[slot],
            device_id={"lat": lat, "lon": target}, device_id_type=MESH)

    sends = [piece_copy(own, lon, 0, mate)] + [piece_copy(own, lon, 1 + i, other(*d)) for i, d in enumerate(peers)]
    for copy in sends:
        copy.start()
    keep_own = pltpu.make_async_copy(own, gathered.at[lon], gat_send.at[n_lon - 1])
    keep_own.start()
    for s in range(2):
        adj_out[s] = adjoint[s]

    for i, d in enumerate(peers):
        slot = other(*d)
        piece_copy(own, slot, 0, mate).wait_recv()
        copy = piece_copy(gathered.at[slot], slot, half + i, mate)
        copy.start()
        sends.append(copy)

    keep_own.wait()
    acc = None
    for pair in range(half):
        first = pair // 2 * 2 + pair % 2 * half
        piece_copy(own, first + 1 - core, 0, mate).wait_recv()
        left = jnp.concatenate([gathered[first], gathered[first + 1]], axis=1)
        term = jnp.dot(left, wide[first * 128:(first + 2) * 128, :], preferred_element_type=f32)
        acc = term if acc is None else acc + term

    for a in range(n_lat):
        partial[a] = acc[:, a * 128:(a + 1) * 128]

    def reduce_copy(d):
        return pltpu.make_async_remote_copy(
            src_ref=partial.at[lax.rem(lat + d, n_lat)], dst_ref=arrived.at[d - 1], send_sem=red_send.at[d - 1],
            recv_sem=red_recv.at[d - 1], device_id=at(d, 0), device_id_type=MESH)

    for d in range(1, n_lat):
        reduce_copy(d).start()
    for copy in halos + sends:
        copy.wait_send()
    total = partial[lat]
    for d in range(1, n_lat):
        reduce_copy(d).wait_recv()
        total = total + arrived[d - 1]
    sum_out[...] = total
    for d in range(1, n_lat):
        reduce_copy(d).wait_send()


def finish(adj, total, adj_out, state_out, flux_out):
    for s in range(2):
        for k in range(8):
            adj_out[s * 8 + k] = pltpu.roll(adj[s], (-16 * k) % 128, 1)[:, 0:16]
    state_out[...] = total[0:16]
    flux_out[...] = total[16:18]


def shards(n_lat, n_lon, forcing, zonal, meridional, mixing, panel):
    def turned(x):
        return jnp.swapaxes(x, -1, -2).reshape((-1, x.shape[-1], x.shape[-2]))

    f32, bf16 = jnp.float32, jnp.bfloat16
    rows = panel.shape[0]
    hbm, vmem = pl.BlockSpec(memory_space=pltpu.HBM), pl.BlockSpec(memory_space=pltpu.VMEM)
    dma = pltpu.SemaphoreType.DMA
    adj, total = pl.pallas_call(
        functools.partial(kernel, n_lat, n_lon),
        out_shape=(jax.ShapeDtypeStruct((2, 8, 128), f32), jax.ShapeDtypeStruct((18, 128), f32)),
        in_specs=[hbm] * 5,
        out_specs=(vmem, vmem),
        scratch_shapes=[
            pltpu.VMEM((55, 8, 16), f32),
            pltpu.VMEM((rows, 8, 128), bf16),
            pltpu.VMEM((6, 8, 128), f32),
            pltpu.VMEM((6, 8, 128), f32),
            pltpu.VMEM((2, 2, 8, 128), f32),
            pltpu.VMEM((128, 1024), bf16),
            pltpu.VMEM((rows, 1024), bf16),
            pltpu.VMEM((18, 128), bf16),
            pltpu.VMEM((n_lon, 18, 128), bf16),
            pltpu.VMEM((n_lat, 18, 128), f32),
            pltpu.VMEM((n_lat - 1, 18, 128), f32),
            dma((4,)), dma((CHUNKS,)), dma((8,)), dma((8,)), dma((n_lon,)), dma((n_lon,)),
            dma((n_lat - 1,)), dma((n_lat - 1,)),
        ],
        compiler_params=pltpu.CompilerParams(
            collective_id=0, has_side_effects=True, vmem_limit_bytes=LIMIT * 1024),
    )(turned(forcing), turned(zonal), turned(meridional), turned(mixing), panel)
    adj, state, flux = pl.pallas_call(
        finish,
        out_shape=(
            jax.ShapeDtypeStruct((16, 8, 16), f32),
            jax.ShapeDtypeStruct((16, 128), f32),
            jax.ShapeDtypeStruct((2, 128), f32),
        ),
        in_specs=[vmem] * 2,
        out_specs=(vmem,) * 3,
        compiler_params=pltpu.CompilerParams(vmem_limit_bytes=1024 * 1024),
    )(adj, total)
    adjoint = jnp.swapaxes(adj.reshape(2, 8, 8, 16), 2, 3)
    return adjoint, state.reshape(2, 8, 1, 128), flux.reshape(2, 1, 128)


def solution(mesh):
    return jax.shard_map(
        functools.partial(shards, mesh.shape["lat"], mesh.shape["lon"]),
        mesh=mesh,
        in_specs=(
            P(None, None, None, "lat", "lon"),
            P(None, "lat", "lon"),
            P(None, "lat", "lon"),
            P(None, "lat", "lon"),
            P("lat", None, "lon"),
        ),
        out_specs=(P(None, None, "lat", "lon"), P(None, None, "lat", "lon"), P(None, "lat", "lon")),
        check_vma=False,
    )
```

```python
import functools

import jax
import jax.numpy as jnp
from jax import lax
from jax.experimental import pallas as pl
from jax.experimental.pallas import tpu as pltpu
from jax.sharding import PartitionSpec as P

MESH = pl.DeviceIdType.MESH
CHUNKS = 8
LIMIT = 55200


def kernel(n_lat, n_lon, forcing, zonal, merid, mixing, panel, adj_out, sum_out,
           raw, pan, msg, halo4, halo8, expand, wide, own, gathered, partial, arrived,
           in_sem, pan_sem, msg_send, msg_recv, gat_send, gat_recv, red_send, red_recv):
    lat, lon = lax.axis_index("lat"), lax.axis_index("lon")
    f32, bf16 = jnp.float32, jnp.bfloat16

    def at(dlat, dlon):
        return {"lat": lax.rem(lat + (dlat + n_lat), n_lat), "lon": lax.rem(lon + (dlon + n_lon), n_lon)}

    half = n_lon // 2
    core, ring, column = lax.rem(lon, 2), lax.rem(lon // 2, half // 2), lon // half

    def other(dz, dy):
        return lax.rem(column + dy, 2) * half + lax.rem(ring + dz, half // 2) * 2 + core

    mate = lon + 1 - 2 * core
    peers = [(dz, dy) for dz in range(half // 2) for dy in range(2) if dz + dy > 0]
    peers = peers[1:] + peers[:1]

    barrier = pltpu.get_barrier_semaphore()
    corners = [(1, 1), (1, -1), (-1, 1), (-1, -1)]
    for dlat, dlon in corners:
        pl.semaphore_signal(barrier, inc=1, device_id=at(dlat, dlon), device_id_type=MESH)
    for d in range(1, n_lat):
        pl.semaphore_signal(barrier, inc=1, device_id=at(d, 0), device_id_type=MESH)
    for target in (lon + 1 - 2 * core, lax.rem(lon + 2 * core - 1 + n_lon, n_lon)):
        pl.semaphore_signal(barrier, inc=1, device_id={"lat": lat, "lon": target}, device_id_type=MESH)
    for dz, dy in peers:
        pl.semaphore_signal(barrier, inc=1, device_id={"lat": lat, "lon": other(dz, dy)}, device_id_type=MESH)

    loads = [
        pltpu.make_async_copy(forcing, raw.at[0:32], in_sem.at[0]),
        pltpu.make_async_copy(zonal, raw.at[32:40], in_sem.at[1]),
        pltpu.make_async_copy(merid, raw.at[40:48], in_sem.at[2]),
        pltpu.make_async_copy(mixing, raw.at[48:55], in_sem.at[3]),
    ]
    for load in loads:
        load.start()
    rows = panel.shape[0] // CHUNKS
    pan_loads = [
        pltpu.make_async_copy(panel.at[i * rows:(i + 1) * rows], pan.at[i * rows:(i + 1) * rows], pan_sem.at[i])
        for i in range(CHUNKS)
    ]
    for load in pan_loads:
        load.start()

    q = lax.broadcasted_iota(jnp.int32, (128, 1024), 0)
    big = lax.broadcasted_iota(jnp.int32, (128, 1024), 1)
    expand[...] = jnp.where((big >> 3) == q, 1.0, 0.0).astype(bf16)
    lane = lax.broadcasted_iota(jnp.int32, (8, 128), 1)
    sub = lax.broadcasted_iota(jnp.int32, (8, 128), 0)
    li = lane & 15
    first_row, last_row = li == 0, li == 15
    first_col, last_col = sub == 0, sub == 7

    for load in loads:
        load.wait()

    def packed(start, count):
        return jnp.concatenate([raw[start + k] for k in range(count)], axis=1)

    zero_level = jnp.zeros((8, 16), f32)
    obs = [packed(0, 8), packed(8, 8)]
    last = [packed(16, 8), packed(24, 8)]
    z = packed(32, 8)
    vm = jnp.where(last_row & (lat == n_lat - 1), 0.0, packed(40, 8))
    mix = jnp.concatenate([raw[48 + k] for k in range(7)] + [zero_level], axis=1)

    def up(x, s):
        return pltpu.roll(x, s % 128, 1)

    def side(x, s):
        return pltpu.roll(x, s % 8, 0)

    def diffuse(x, m):
        flow = m * (up(x, -16) - x)
        return x + flow - up(flow, 16)

    g = [diffuse(x, mix) for x in last]
    mine = g + [z, vm] + obs + [mix]

    def pack_rows(top):
        total = jnp.zeros((8, 128), f32)
        for n, x in enumerate(mine):
            total = jnp.where((li >> 1) == n, up(x, 2 * n - (14 if top else 0)), total)
        return total

    def pack_cols(right, fields):
        total = jnp.zeros((8, 128), f32)
        for n, x in enumerate(fields):
            total = jnp.where((sub >> 1) == n, side(x, 2 * n - (6 if right else 0)), total)
        return total

    msg[0] = pack_rows(True)
    msg[1] = pack_rows(False)
    msg[2] = pack_cols(True, mine[:4])
    msg[3] = pack_cols(True, mine[4:])
    msg[4] = pack_cols(False, mine[:4])
    msg[5] = pack_cols(False, mine[4:])

    pl.semaphore_wait(barrier, (n_lat - 1) + (half + 1) + 4)

    def row_copy(slot, kind, dlat, dlon):
        return pltpu.make_async_remote_copy(
            src_ref=msg.at[kind], dst_ref=halo4.at[slot], send_sem=msg_send.at[slot], recv_sem=msg_recv.at[slot],
            device_id=at(dlat, dlon), device_id_type=MESH)

    def col_copy(slot, kind, dlon):
        return pltpu.make_async_remote_copy(
            src_ref=msg.at[kind:kind + 2], dst_ref=halo8.at[slot], send_sem=msg_send.at[6 + slot],
            recv_sem=msg_recv.at[6 + slot], device_id=at(0, dlon), device_id_type=MESH)

    halos = [
        row_copy(0, 1, -1, 0), row_copy(3, 0, 1, 0), col_copy(0, 4, -1), col_copy(1, 2, 1),
        row_copy(1, 1, -1, -1), row_copy(2, 1, -1, 1), row_copy(4, 0, 1, -1), row_copy(5, 0, 1, 1),
    ]
    for copy in halos:
        copy.start()

    def relayout(begin, end):
        for i in range(begin, end):
            pan_loads[i].wait()

            def turn(j, carry):
                at_row = i * rows + j * 128
                wide[pl.ds(at_row, 128), :] = pan[pl.ds(at_row, 128)].reshape(128, 1024)
                return carry

            lax.fori_loop(0, rows // 128, turn, 0)

    def advect(x, north, south, east, west, c):
        p, nw, qn, ns = c
        return x * (1.0 - p + nw - qn + ns) + east * p - west * nw + north * qn - south * ns

    def coefs(zc, z_west, v, v_south):
        return (jnp.maximum(zc, 0.0), jnp.minimum(z_west, 0.0), jnp.maximum(v, 0.0), jnp.minimum(v_south, 0.0))

    relayout(0, CHUNKS)

    for copy in halos:
        copy.wait_recv()

    def rows_of(slot, n, north):
        return up(halo4[slot], -2 * n if north else 14 - 2 * n)

    def cols_of(slot, n):
        return side(halo8[slot, n // 4], -2 * (n % 4) if slot == 0 else 6 - 2 * (n % 4))

    N = [rows_of(0, n, True) for n in range(7)]
    S = [rows_of(3, n, False) for n in range(7)]
    NE = [rows_of(1, n, True) for n in range(4)]
    NW = [rows_of(2, n, True) for n in range(4)]
    SE = [rows_of(4, n, False) for n in range(4)]
    SW = [rows_of(5, n, False) for n in range(4)]
    E = [cols_of(0, n) for n in range(7)]
    W = [cols_of(1, n) for n in range(7)]

    def north_of(x, xn):
        return jnp.where(last_row, up(xn, 15), up(x, -1))

    def south_of(x, xs):
        return jnp.where(first_row, up(xs, -15), up(x, 1))

    def east_of(x, xe):
        return side(jnp.where(first_col, xe, x), -1)

    def west_of(x, xw):
        return side(jnp.where(last_col, xw, x), 1)

    def middle(me, n_, s_, e_, w_):
        c = coefs(me[2], west_of(me[2], w_[2]), me[3], south_of(me[3], s_[3]))
        return c, [
            advect(me[s], north_of(me[s], n_[s]), south_of(me[s], s_[s]), east_of(me[s], e_[s]), west_of(me[s], w_[s]), c)
            + me[4 + s]
            for s in range(2)
        ]

    coef, mid = middle(mine, N, S, E, W)
    mid_n = middle(N, N, mine, NE, NW)[1]
    mid_s = middle(S, mine, S, SE, SW)[1]
    mid_e = middle(E, NE, SE, E, mine)[1]
    mid_w = middle(W, NW, SW, mine, W)[1]
    surface = [last[s] + mid[s] for s in range(2)]
    adjoint = []
    for s in range(2):
        d = diffuse(mid[s], mix)
        dn, ds = diffuse(mid_n[s], N[6]), diffuse(mid_s[s], S[6])
        de, dw = diffuse(mid_e[s], E[6]), diffuse(mid_w[s], W[6])
        adjoint.append(advect(d, north_of(d, dn), south_of(d, ds), east_of(d, de), west_of(d, dw), coef))

    x = jnp.concatenate([adjoint[0], adjoint[1]], axis=0).astype(bf16)
    y = jnp.dot(x, expand[...], preferred_element_type=f32)
    xs = jnp.concatenate(surface, axis=0).astype(bf16)
    ys = jnp.dot(xs, expand[:, 0:128], preferred_element_type=f32)
    keep = (lax.broadcasted_iota(jnp.int32, (16, 128), 1) & 7) == (lax.broadcasted_iota(jnp.int32, (16, 128), 0) & 7)
    blocks = [jnp.where(keep, y[:, k * 128:(k + 1) * 128], 0.0).astype(bf16) for k in range(8)]
    stacked = jnp.concatenate(blocks, axis=0)
    c_row = lax.broadcasted_iota(jnp.int32, (18, 128), 0)
    c_col = lax.broadcasted_iota(jnp.int32, (18, 128), 1)
    pick = (c_row < 16) & ((c_col >> 4) == (c_row & 7)) & (((c_col >> 3) & 1) == (c_row >> 3))
    f_row = lax.broadcasted_iota(jnp.int32, (18, 16), 0)
    f_col = lax.broadcasted_iota(jnp.int32, (18, 16), 1)
    pick_f = (f_col >> 3) == (f_row - 16)
    vec = jnp.dot(jnp.where(pick, 1.0, 0.0).astype(bf16), stacked, preferred_element_type=f32)
    vec = vec + jnp.dot(
        jnp.where(pick_f, 1.0, 0.0).astype(bf16), jnp.where(keep, ys, 0.0).astype(bf16), preferred_element_type=f32)
    own[...] = vec.astype(bf16)

    def piece_copy(source, slot, send, target):
        return pltpu.make_async_remote_copy(
            src_ref=source, dst_ref=gathered.at[slot], send_sem=gat_send.at[send], recv_sem=gat_recv.at[slot],
            device_id={"lat": lat, "lon": target}, device_id_type=MESH)

    near = [d for d in peers if d[0] == 0]
    far = [d for d in peers if d not in near]
    targets = [mate]
    for d in near:
        targets += [other(*d), other(*d) + 1 - 2 * core]
    targets += [other(*d) for d in far]
    sends = [piece_copy(own, lon, i, target) for i, target in enumerate(targets)]
    for copy in sends:
        copy.start()
    keep_own = pltpu.make_async_copy(own, gathered.at[lon], gat_send.at[n_lon - 1])
    keep_own.start()
    for s in range(2):
        adj_out[s] = adjoint[s]

    for d in far:
        slot = other(*d)
        piece_copy(own, slot, 0, mate).wait_recv()
        copy = piece_copy(gathered.at[slot], slot, len(sends), mate)
        copy.start()
        sends.append(copy)
    for d in near:
        piece_copy(own, other(*d), 0, mate).wait_recv()

    keep_own.wait()
    acc = None
    for pair in range(half):
        first = pair // 2 * 2 + pair % 2 * half
        piece_copy(own, first + 1 - core, 0, mate).wait_recv()
        left = jnp.concatenate([gathered[first], gathered[first + 1]], axis=1)
        term = jnp.dot(left, wide[first * 128:(first + 2) * 128, :], preferred_element_type=f32)
        acc = term if acc is None else acc + term

    for a in range(n_lat):
        partial[a] = acc[:, a * 128:(a + 1) * 128]

    def reduce_copy(d):
        return pltpu.make_async_remote_copy(
            src_ref=partial.at[lax.rem(lat + d, n_lat)], dst_ref=arrived.at[d - 1], send_sem=red_send.at[d - 1],
            recv_sem=red_recv.at[d - 1], device_id=at(d, 0), device_id_type=MESH)

    for d in range(1, n_lat):
        reduce_copy(d).start()
    for copy in halos + sends:
        copy.wait_send()
    total = partial[lat]
    for d in range(1, n_lat):
        reduce_copy(d).wait_recv()
        total = total + arrived[d - 1]
    sum_out[...] = total
    for d in range(1, n_lat):
        reduce_copy(d).wait_send()


def finish(adj, total, adj_out, state_out, flux_out):
    for s in range(2):
        for k in range(8):
            adj_out[s * 8 + k] = pltpu.roll(adj[s], (-16 * k) % 128, 1)[:, 0:16]
    state_out[...] = total[0:16]
    flux_out[...] = total[16:18]


def shards(n_lat, n_lon, forcing, zonal, meridional, mixing, panel):
    def turned(x):
        return jnp.swapaxes(x, -1, -2).reshape((-1, x.shape[-1], x.shape[-2]))

    f32, bf16 = jnp.float32, jnp.bfloat16
    rows = panel.shape[0]
    hbm, vmem = pl.BlockSpec(memory_space=pltpu.HBM), pl.BlockSpec(memory_space=pltpu.VMEM)
    dma = pltpu.SemaphoreType.DMA
    adj, total = pl.pallas_call(
        functools.partial(kernel, n_lat, n_lon),
        out_shape=(jax.ShapeDtypeStruct((2, 8, 128), f32), jax.ShapeDtypeStruct((18, 128), f32)),
        in_specs=[hbm] * 5,
        out_specs=(vmem, vmem),
        scratch_shapes=[
            pltpu.VMEM((55, 8, 16), f32),
            pltpu.VMEM((rows, 8, 128), bf16),
            pltpu.VMEM((6, 8, 128), f32),
            pltpu.VMEM((6, 8, 128), f32),
            pltpu.VMEM((2, 2, 8, 128), f32),
            pltpu.VMEM((128, 1024), bf16),
            pltpu.VMEM((rows, 1024), bf16),
            pltpu.VMEM((18, 128), bf16),
            pltpu.VMEM((n_lon, 18, 128), bf16),
            pltpu.VMEM((n_lat, 18, 128), f32),
            pltpu.VMEM((n_lat - 1, 18, 128), f32),
            dma((4,)), dma((CHUNKS,)), dma((8,)), dma((8,)), dma((n_lon,)), dma((n_lon,)),
            dma((n_lat - 1,)), dma((n_lat - 1,)),
        ],
        compiler_params=pltpu.CompilerParams(
            collective_id=0, has_side_effects=True, vmem_limit_bytes=LIMIT * 1024),
    )(turned(forcing), turned(zonal), turned(meridional), turned(mixing), panel)
    adj, state, flux = pl.pallas_call(
        finish,
        out_shape=(
            jax.ShapeDtypeStruct((16, 8, 16), f32),
            jax.ShapeDtypeStruct((16, 128), f32),
            jax.ShapeDtypeStruct((2, 128), f32),
        ),
        in_specs=[vmem] * 2,
        out_specs=(vmem,) * 3,
        compiler_params=pltpu.CompilerParams(vmem_limit_bytes=1024 * 1024),
    )(adj, total)
    adjoint = jnp.swapaxes(adj.reshape(2, 8, 8, 16), 2, 3)
    return adjoint, state.reshape(2, 8, 1, 128), flux.reshape(2, 1, 128)


def solution(mesh):
    return jax.shard_map(
        functools.partial(shards, mesh.shape["lat"], mesh.shape["lon"]),
        mesh=mesh,
        in_specs=(
            P(None, None, None, "lat", "lon"),
            P(None, "lat", "lon"),
            P(None, "lat", "lon"),
            P(None, "lat", "lon"),
            P("lat", None, "lon"),
        ),
        out_specs=(P(None, None, "lat", "lon"), P(None, None, "lat", "lon"), P(None, "lat", "lon")),
        check_vma=False,
    )
```

```python
import functools

import jax
import jax.numpy as jnp
from jax import lax
from jax.experimental import pallas as pl
from jax.experimental.pallas import tpu as pltpu
from jax.sharding import PartitionSpec as P

MESH = pl.DeviceIdType.MESH
CHUNKS = 8
LIMIT = 55200


def kernel(n_lat, n_lon, forcing, zonal, merid, mixing, panel, adj_out, sum_out,
           raw, pan, msg, halo4, halo8, expand, wide, own, gathered, partial, arrived,
           in_sem, pan_sem, msg_send, msg_recv, gat_send, gat_recv, red_send, red_recv):
    lat, lon = lax.axis_index("lat"), lax.axis_index("lon")
    f32, bf16 = jnp.float32, jnp.bfloat16

    def at(dlat, dlon):
        return {"lat": lax.rem(lat + (dlat + n_lat), n_lat), "lon": lax.rem(lon + (dlon + n_lon), n_lon)}

    half = n_lon // 2
    core, ring, column = lax.rem(lon, 2), lax.rem(lon // 2, half // 2), lon // half

    def other(dz, dy):
        return lax.rem(column + dy, 2) * half + lax.rem(ring + dz, half // 2) * 2 + core

    mate = lon + 1 - 2 * core
    peers = [(dz, dy) for dz in range(half // 2) for dy in (1, 0) if dz + dy > 0]

    barrier = pltpu.get_barrier_semaphore()
    corners = [(1, 1), (1, -1), (-1, 1), (-1, -1)]
    for dlat, dlon in corners:
        pl.semaphore_signal(barrier, inc=1, device_id=at(dlat, dlon), device_id_type=MESH)
    for d in range(1, n_lat):
        pl.semaphore_signal(barrier, inc=1, device_id=at(d, 0), device_id_type=MESH)
    for target in (lon + 1 - 2 * core, lax.rem(lon + 2 * core - 1 + n_lon, n_lon)):
        pl.semaphore_signal(barrier, inc=1, device_id={"lat": lat, "lon": target}, device_id_type=MESH)
    for dz, dy in peers:
        pl.semaphore_signal(barrier, inc=1, device_id={"lat": lat, "lon": other(dz, dy)}, device_id_type=MESH)

    loads = [
        pltpu.make_async_copy(forcing, raw.at[0:32], in_sem.at[0]),
        pltpu.make_async_copy(zonal, raw.at[32:40], in_sem.at[1]),
        pltpu.make_async_copy(merid, raw.at[40:48], in_sem.at[2]),
        pltpu.make_async_copy(mixing, raw.at[48:55], in_sem.at[3]),
    ]
    for load in loads:
        load.start()
    rows = panel.shape[0] // CHUNKS
    pan_loads = [
        pltpu.make_async_copy(panel.at[i * rows:(i + 1) * rows], pan.at[i * rows:(i + 1) * rows], pan_sem.at[i])
        for i in range(CHUNKS)
    ]
    for load in pan_loads:
        load.start()

    q = lax.broadcasted_iota(jnp.int32, (128, 1024), 0)
    big = lax.broadcasted_iota(jnp.int32, (128, 1024), 1)
    expand[...] = jnp.where((big >> 3) == q, 1.0, 0.0).astype(bf16)
    lane = lax.broadcasted_iota(jnp.int32, (8, 128), 1)
    sub = lax.broadcasted_iota(jnp.int32, (8, 128), 0)
    li = lane & 15
    first_row, last_row = li == 0, li == 15
    first_col, last_col = sub == 0, sub == 7

    for load in loads:
        load.wait()

    def packed(start, count):
        return jnp.concatenate([raw[start + k] for k in range(count)], axis=1)

    zero_level = jnp.zeros((8, 16), f32)
    obs = [packed(0, 8), packed(8, 8)]
    last = [packed(16, 8), packed(24, 8)]
    z = packed(32, 8)
    vm = jnp.where(last_row & (lat == n_lat - 1), 0.0, packed(40, 8))
    mix = jnp.concatenate([raw[48 + k] for k in range(7)] + [zero_level], axis=1)

    def up(x, s):
        return pltpu.roll(x, s % 128, 1)

    def side(x, s):
        return pltpu.roll(x, s % 8, 0)

    def diffuse(x, m):
        flow = m * (up(x, -16) - x)
        return x + flow - up(flow, 16)

    g = [diffuse(x, mix) for x in last]
    mine = g + [z, vm] + obs + [mix]

    def pack_rows(top):
        total = jnp.zeros((8, 128), f32)
        for n, x in enumerate(mine):
            total = jnp.where((li >> 1) == n, up(x, 2 * n - (14 if top else 0)), total)
        return total

    def pack_cols(right, fields):
        total = jnp.zeros((8, 128), f32)
        for n, x in enumerate(fields):
            total = jnp.where((sub >> 1) == n, side(x, 2 * n - (6 if right else 0)), total)
        return total

    msg[0] = pack_rows(True)
    msg[1] = pack_rows(False)
    msg[2] = pack_cols(True, mine[:4])
    msg[3] = pack_cols(True, mine[4:])
    msg[4] = pack_cols(False, mine[:4])
    msg[5] = pack_cols(False, mine[4:])

    pl.semaphore_wait(barrier, (n_lat - 1) + (half + 1) + 4)

    def row_copy(slot, kind, dlat, dlon):
        return pltpu.make_async_remote_copy(
            src_ref=msg.at[kind], dst_ref=halo4.at[slot], send_sem=msg_send.at[slot], recv_sem=msg_recv.at[slot],
            device_id=at(dlat, dlon), device_id_type=MESH)

    def col_copy(slot, kind, dlon):
        return pltpu.make_async_remote_copy(
            src_ref=msg.at[kind:kind + 2], dst_ref=halo8.at[slot], send_sem=msg_send.at[6 + slot],
            recv_sem=msg_recv.at[6 + slot], device_id=at(0, dlon), device_id_type=MESH)

    halos = [
        row_copy(1, 1, -1, -1), row_copy(2, 1, -1, 1), row_copy(4, 0, 1, -1), row_copy(5, 0, 1, 1),
        row_copy(0, 1, -1, 0), row_copy(3, 0, 1, 0), col_copy(0, 4, -1), col_copy(1, 2, 1),
    ]
    for copy in halos:
        copy.start()

    def relayout(begin, end):
        for i in range(begin, end):
            pan_loads[i].wait()

            def turn(j, carry):
                at_row = i * rows + j * 128
                wide[pl.ds(at_row, 128), :] = pan[pl.ds(at_row, 128)].reshape(128, 1024)
                return carry

            lax.fori_loop(0, rows // 128, turn, 0)

    def advect(x, north, south, east, west, c):
        p, nw, qn, ns = c
        return x * (1.0 - p + nw - qn + ns) + east * p - west * nw + north * qn - south * ns

    def coefs(zc, z_west, v, v_south):
        return (jnp.maximum(zc, 0.0), jnp.minimum(z_west, 0.0), jnp.maximum(v, 0.0), jnp.minimum(v_south, 0.0))

    relayout(0, CHUNKS)

    for copy in halos:
        copy.wait_recv()

    def rows_of(slot, n, north):
        return up(halo4[slot], -2 * n if north else 14 - 2 * n)

    def cols_of(slot, n):
        return side(halo8[slot, n // 4], -2 * (n % 4) if slot == 0 else 6 - 2 * (n % 4))

    N = [rows_of(0, n, True) for n in range(7)]
    S = [rows_of(3, n, False) for n in range(7)]
    NE = [rows_of(1, n, True) for n in range(4)]
    NW = [rows_of(2, n, True) for n in range(4)]
    SE = [rows_of(4, n, False) for n in range(4)]
    SW = [rows_of(5, n, False) for n in range(4)]
    E = [cols_of(0, n) for n in range(7)]
    W = [cols_of(1, n) for n in range(7)]

    def north_of(x, xn):
        return jnp.where(last_row, up(xn, 15), up(x, -1))

    def south_of(x, xs):
        return jnp.where(first_row, up(xs, -15), up(x, 1))

    def east_of(x, xe):
        return side(jnp.where(first_col, xe, x), -1)

    def west_of(x, xw):
        return side(jnp.where(last_col, xw, x), 1)

    def middle(me, n_, s_, e_, w_):
        c = coefs(me[2], west_of(me[2], w_[2]), me[3], south_of(me[3], s_[3]))
        return c, [
            advect(me[s], north_of(me[s], n_[s]), south_of(me[s], s_[s]), east_of(me[s], e_[s]), west_of(me[s], w_[s]), c)
            + me[4 + s]
            for s in range(2)
        ]

    coef, mid = middle(mine, N, S, E, W)
    mid_n = middle(N, N, mine, NE, NW)[1]
    mid_s = middle(S, mine, S, SE, SW)[1]
    mid_e = middle(E, NE, SE, E, mine)[1]
    mid_w = middle(W, NW, SW, mine, W)[1]
    surface = [last[s] + mid[s] for s in range(2)]
    adjoint = []
    for s in range(2):
        d = diffuse(mid[s], mix)
        dn, ds = diffuse(mid_n[s], N[6]), diffuse(mid_s[s], S[6])
        de, dw = diffuse(mid_e[s], E[6]), diffuse(mid_w[s], W[6])
        adjoint.append(advect(d, north_of(d, dn), south_of(d, ds), east_of(d, de), west_of(d, dw), coef))

    x = jnp.concatenate([adjoint[0], adjoint[1]], axis=0).astype(bf16)
    y = jnp.dot(x, expand[...], preferred_element_type=f32)
    xs = jnp.concatenate(surface, axis=0).astype(bf16)
    ys = jnp.dot(xs, expand[:, 0:128], preferred_element_type=f32)
    keep = (lax.broadcasted_iota(jnp.int32, (16, 128), 1) & 7) == (lax.broadcasted_iota(jnp.int32, (16, 128), 0) & 7)
    blocks = [jnp.where(keep, y[:, k * 128:(k + 1) * 128], 0.0).astype(bf16) for k in range(8)]
    stacked = jnp.concatenate(blocks, axis=0)
    c_row = lax.broadcasted_iota(jnp.int32, (18, 128), 0)
    c_col = lax.broadcasted_iota(jnp.int32, (18, 128), 1)
    pick = (c_row < 16) & ((c_col >> 4) == (c_row & 7)) & (((c_col >> 3) & 1) == (c_row >> 3))
    f_row = lax.broadcasted_iota(jnp.int32, (18, 16), 0)
    f_col = lax.broadcasted_iota(jnp.int32, (18, 16), 1)
    pick_f = (f_col >> 3) == (f_row - 16)
    vec = jnp.dot(jnp.where(pick, 1.0, 0.0).astype(bf16), stacked, preferred_element_type=f32)
    vec = vec + jnp.dot(
        jnp.where(pick_f, 1.0, 0.0).astype(bf16), jnp.where(keep, ys, 0.0).astype(bf16), preferred_element_type=f32)
    own[...] = vec.astype(bf16)

    def piece_copy(source, slot, send, target):
        return pltpu.make_async_remote_copy(
            src_ref=source, dst_ref=gathered.at[slot], send_sem=gat_send.at[send], recv_sem=gat_recv.at[slot],
            device_id={"lat": lat, "lon": target}, device_id_type=MESH)

    near = [d for d in peers if d[0] == 0]
    far = [d for d in peers if d not in near]
    by_far = sorted(far, key=lambda d: -min(d[0], half // 2 - d[0]))
    targets = [mate]
    for d in near:
        targets += [other(*d), other(*d) + 1 - 2 * core]
    targets += [other(*d) for d in by_far]
    sends = [piece_copy(own, lon, i, target) for i, target in enumerate(targets)]
    for copy in sends:
        copy.start()
    keep_own = pltpu.make_async_copy(own, gathered.at[lon], gat_send.at[n_lon - 1])
    keep_own.start()
    for s in range(2):
        adj_out[s] = adjoint[s]

    for d in far:
        slot = other(*d)
        piece_copy(own, slot, 0, mate).wait_recv()
        copy = piece_copy(gathered.at[slot], slot, len(sends), mate)
        copy.start()
        sends.append(copy)
    for d in near:
        piece_copy(own, other(*d), 0, mate).wait_recv()

    keep_own.wait()
    acc = None
    for pair in range(half):
        first = pair // 2 * 2 + pair % 2 * half
        piece_copy(own, first + 1 - core, 0, mate).wait_recv()
        left = jnp.concatenate([gathered[first], gathered[first + 1]], axis=1)
        term = jnp.dot(left, wide[first * 128:(first + 2) * 128, :], preferred_element_type=f32)
        acc = term if acc is None else acc + term

    for a in range(n_lat):
        partial[a] = acc[:, a * 128:(a + 1) * 128]

    def reduce_copy(d):
        return pltpu.make_async_remote_copy(
            src_ref=partial.at[lax.rem(lat + d, n_lat)], dst_ref=arrived.at[d - 1], send_sem=red_send.at[d - 1],
            recv_sem=red_recv.at[d - 1], device_id=at(d, 0), device_id_type=MESH)

    for d in sorted(range(1, n_lat), key=lambda d: -min(d, n_lat - d)):
        reduce_copy(d).start()
    for copy in halos + sends:
        copy.wait_send()
    total = partial[lat]
    for d in range(1, n_lat):
        reduce_copy(d).wait_recv()
        total = total + arrived[d - 1]
    sum_out[...] = total
    for d in range(1, n_lat):
        reduce_copy(d).wait_send()


def finish(adj, total, adj_out, state_out, flux_out):
    for s in range(2):
        for k in range(8):
            adj_out[s * 8 + k] = pltpu.roll(adj[s], (-16 * k) % 128, 1)[:, 0:16]
    state_out[...] = total[0:16]
    flux_out[...] = total[16:18]


def shards(n_lat, n_lon, forcing, zonal, meridional, mixing, panel):
    def turned(x):
        return jnp.swapaxes(x, -1, -2).reshape((-1, x.shape[-1], x.shape[-2]))

    f32, bf16 = jnp.float32, jnp.bfloat16
    rows = panel.shape[0]
    hbm, vmem = pl.BlockSpec(memory_space=pltpu.HBM), pl.BlockSpec(memory_space=pltpu.VMEM)
    dma = pltpu.SemaphoreType.DMA
    adj, total = pl.pallas_call(
        functools.partial(kernel, n_lat, n_lon),
        out_shape=(jax.ShapeDtypeStruct((2, 8, 128), f32), jax.ShapeDtypeStruct((18, 128), f32)),
        in_specs=[hbm] * 5,
        out_specs=(vmem, vmem),
        scratch_shapes=[
            pltpu.VMEM((55, 8, 16), f32),
            pltpu.VMEM((rows, 8, 128), bf16),
            pltpu.VMEM((6, 8, 128), f32),
            pltpu.VMEM((6, 8, 128), f32),
            pltpu.VMEM((2, 2, 8, 128), f32),
            pltpu.VMEM((128, 1024), bf16),
            pltpu.VMEM((rows, 1024), bf16),
            pltpu.VMEM((18, 128), bf16),
            pltpu.VMEM((n_lon, 18, 128), bf16),
            pltpu.VMEM((n_lat, 18, 128), f32),
            pltpu.VMEM((n_lat - 1, 18, 128), f32),
            dma((4,)), dma((CHUNKS,)), dma((8,)), dma((8,)), dma((n_lon,)), dma((n_lon,)),
            dma((n_lat - 1,)), dma((n_lat - 1,)),
        ],
        compiler_params=pltpu.CompilerParams(
            collective_id=0, has_side_effects=True, vmem_limit_bytes=LIMIT * 1024),
    )(turned(forcing), turned(zonal), turned(meridional), turned(mixing), panel)
    adj, state, flux = pl.pallas_call(
        finish,
        out_shape=(
            jax.ShapeDtypeStruct((16, 8, 16), f32),
            jax.ShapeDtypeStruct((16, 128), f32),
            jax.ShapeDtypeStruct((2, 128), f32),
        ),
        in_specs=[vmem] * 2,
        out_specs=(vmem,) * 3,
        compiler_params=pltpu.CompilerParams(vmem_limit_bytes=1024 * 1024),
    )(adj, total)
    adjoint = jnp.swapaxes(adj.reshape(2, 8, 8, 16), 2, 3)
    return adjoint, state.reshape(2, 8, 1, 128), flux.reshape(2, 1, 128)


def solution(mesh):
    return jax.shard_map(
        functools.partial(shards, mesh.shape["lat"], mesh.shape["lon"]),
        mesh=mesh,
        in_specs=(
            P(None, None, None, "lat", "lon"),
            P(None, "lat", "lon"),
            P(None, "lat", "lon"),
            P(None, "lat", "lon"),
            P("lat", None, "lon"),
        ),
        out_specs=(P(None, None, "lat", "lon"), P(None, None, "lat", "lon"), P(None, "lat", "lon")),
        check_vma=False,
    )
```
